32 devices in a mesh: tile: 8 (over z, y), slab: 4 (over x, core).
Axes of the slice: x: 2, y: 2, z: 4, core: 2. Of those that a mesh axis runs over, the one named last changes fastest.
Arguments:
- incident: float32 [2, 1024, 128], P(None, 'tile'), may hold values from -6 to 6
- target: float32 [2, 1024, 128], P(None, 'tile'), may hold values from -6 to 6
- kernel: float32 [2, 33], replicated, may hold values from -0.25 to 0.25
- phase_screen: float32 [8, 1024, 128], P('slab', 'tile'), may hold values from -1.5 to 1.5
- plane_shift: int32 [8], P('slab'), may hold values from -8 to 8, as said below
- slab_planes: int32 [4], P('slab'), may hold values from 1 to 2, 6 in all
Outputs:
- gradient: float32 [8, 1024, 128], P('slab', 'tile')
The draws below stay inside these ranges and needn't reach their ends.
Inputs may be any that keep to these rules, and one draw needn't show every extreme that they name: `plane_shift`: some plane's shift is exactly 8 and another plane's is exactly minus 8. `slab_planes`: the counts sum to 6, and some slab has exactly 2 live planes; a slab's live planes are its first ones.
All inputs are finite; a program needn't handle non-finite values. No bound on the sum of `slab_planes` on one device may be relied on, other than what follows from the above.
Results may differ from the reference program's by a relative error of at most 0.0003.
Values sent between devices are 32-bit elements; how exact they have to be, the bound alone decides.
A program may use at most 64 MiB of HBM per device.

```python
import math
import jax
import jax.numpy as jnp
import numpy as np
from jax import lax

COLS_DEV = 128
PLANES_DEV = 2
TILT_MAX = 8
TAPS = 33
GRID_ROWS = 1024
PLANES_ALL = 8
PLANES_USED = 6
N_SLAB = 4


def draw_kernel(key, part):
    chirp_key = jax.random.fold_in(key, 21)
    noise_key = jax.random.fold_in(key, 22)
    chirp_scale = jax.random.uniform(chirp_key, (), jnp.float32, 28.0, 36.0)
    offsets = jnp.arange(TAPS, dtype=jnp.float32) - TAPS // 2
    window = 0.75 + 0.25 * jnp.cos(jnp.pi * offsets / (TAPS // 2 + 1))
    angle_values = jnp.pi * offsets * offsets / chirp_scale
    amplitude = window / jnp.sqrt(chirp_scale)
    noise = jnp.clip(0.01 * jax.random.normal(noise_key, (2, TAPS), jnp.float32), -0.03, 0.03)
    taps = jnp.stack([amplitude * jnp.cos(angle_values), amplitude * jnp.sin(angle_values)]) + noise
    return taps.astype(jnp.float32)


def draw_plane_shift(key, part):
    shift_key = jax.random.fold_in(key, 11)
    high_key = jax.random.fold_in(key, 12)
    low_key = jax.random.fold_in(key, 13)
    shift_values = jax.random.randint(shift_key, (PLANES_ALL,), -TILT_MAX, TILT_MAX + 1)
    high_slot = jax.random.randint(high_key, (), 0, PLANES_ALL)
    low_slot = (high_slot + 1 + jax.random.randint(low_key, (), 0, PLANES_ALL - 1)) % PLANES_ALL
    positions = jnp.arange(PLANES_ALL)
    shift_values = jnp.where(positions == high_slot, TILT_MAX, shift_values)
    shift_values = jnp.where(positions == low_slot, -TILT_MAX, shift_values)
    return shift_values.astype(jnp.int32)


def level_of(own_key, shape, shards, least, largest):
    gain, own = 1.0, jax.random.fold_in(own_key, 6)
    for position, parts in shards:
        steps = jnp.exp(jax.random.uniform(jax.random.fold_in(own, position), (parts,), jnp.float32, least / len(shards), largest / len(shards)))
        gain = gain * jnp.repeat(steps, shape[position] // parts).reshape([-1 if axis == position else 1 for axis in range(len(shape))])
    return gain


def split_up(count, total, limit, lean):
    loads = [(1 << 20) // math.isqrt(grade ** lean) + 1 for grade in range(2, count + 1)]
    rest, given = total - limit - (count - 1), [1] * (count - 1)
    while rest > 0:
        movable = [i for i in range(count - 1) if given[i] < limit]
        mass, remaining = sum([loads[i] for i in movable]), rest
        for i in movable:
            addition = min(limit - given[i], max(1, remaining * loads[i] // mass), rest)
            given[i] = given[i] + addition
            rest = rest - addition
    return np.array([limit] + given)


def uneven(own_key, count, total, reach, slope):
    if count == 2:
        one = jax.random.randint(own_key, (), max(1, total - reach), min(reach, total - 1) + 1)
        return jnp.stack([one, total - one])
    sizes = jnp.asarray(split_up(count, total, reach, slope), jnp.int32)
    pairs = (count - 1) // 2
    giver, receiver = sizes[1:1 + 2 * pairs:2], sizes[2:2 + 2 * pairs:2]
    room = jnp.minimum(giver - 1, reach - receiver)
    moved = jax.random.randint(jax.random.fold_in(own_key, 1), (pairs,), 0, 1 << 20) % (room + 1)
    sizes = sizes.at[1:1 + 2 * pairs:2].set(giver - moved).at[2:2 + 2 * pairs:2].set(receiver + moved)
    return sizes[jax.random.permutation(jax.random.fold_in(own_key, 2), count)]


def scatter_about(stream_key, dims, scale, limit, split=(), kind=jnp.bfloat16):
    entries = jax.random.normal(stream_key, dims, jnp.float32) * scale
    if len(split) > 0:
        entries = level_of(stream_key, dims, split, -0.22, 0.18) * entries
    return jnp.clip(entries, min=-limit, max=limit).astype(kind)


def setup_inputs(seed: int = 0) -> dict:
    keys = jax.random.split(jax.random.key(seed), 7)
    incident = scatter_about(keys[0], (2, GRID_ROWS, COLS_DEV), 1.0, 6.0, ((1, 8),), jnp.float32)
    target = scatter_about(keys[1], (2, GRID_ROWS, COLS_DEV), 1.0, 6.0, ((1, 8),), jnp.float32)
    kernel = draw_kernel(jax.random.fold_in(keys[6], 71), 0)
    phase_screen = jnp.clip(jax.random.uniform(keys[3], (PLANES_ALL, GRID_ROWS, COLS_DEV), jnp.float32, -1.5, 1.5) * level_of(keys[3], (PLANES_ALL, GRID_ROWS, COLS_DEV), ((0, 4), (1, 8)), -0.4, 0.0), -1.5, 1.5)
    plane_shift = draw_plane_shift(jax.random.fold_in(keys[6], 71), 0)
    slab_planes = uneven(keys[5], N_SLAB, PLANES_USED, PLANES_DEV, 0).astype(jnp.int32)
    return {"incident": incident, "target": target, "kernel": kernel, "phase_screen": phase_screen, "plane_shift": plane_shift, "slab_planes": slab_planes}


tap_reach = 16

def spread_rows(field_in, kernel, shift_rows):
    margin = tap_reach + TILT_MAX
    padded = jnp.pad(field_in, ((0, 0), (margin, margin), (0, 0)))
    real_part = jnp.zeros((GRID_ROWS, COLS_DEV), jnp.float32)
    imag_part = jnp.zeros((GRID_ROWS, COLS_DEV), jnp.float32)
    for tap_index in range(2 * tap_reach + 1):
        start_row = shift_rows + (margin + tap_index - tap_reach)
        window_rows = lax.dynamic_slice_in_dim(padded, start_row, GRID_ROWS, axis=1)
        real_part = real_part + kernel[0, tap_index] * window_rows[0] - kernel[1, tap_index] * window_rows[1]
        imag_part = imag_part + kernel[0, tap_index] * window_rows[1] + kernel[1, tap_index] * window_rows[0]
    return jnp.stack([real_part, imag_part])

def spread_cols(field_in, kernel):
    padded = jnp.pad(field_in, ((0, 0), (0, 0), (tap_reach, tap_reach)))
    real_part = jnp.zeros((GRID_ROWS, COLS_DEV), jnp.float32)
    imag_part = jnp.zeros((GRID_ROWS, COLS_DEV), jnp.float32)
    for tap_index in range(2 * tap_reach + 1):
        window_cols = padded[:, :, tap_index:tap_index + COLS_DEV]
        real_part = real_part + kernel[0, tap_index] * window_cols[0] - kernel[1, tap_index] * window_cols[1]
        imag_part = imag_part + kernel[0, tap_index] * window_cols[1] + kernel[1, tap_index] * window_cols[0]
    return jnp.stack([real_part, imag_part])

def exit_field(phase_screen, incident, kernel, plane_shift, slab_planes):
    current = incident
    for slab_index in range(N_SLAB):
        for plane_index in range(PLANES_DEV):
            layer_index = slab_index * PLANES_DEV + plane_index
            spread = spread_cols(spread_rows(current, kernel, plane_shift[layer_index]), kernel)
            cosine_part = jnp.cos(phase_screen[layer_index])
            sine_part = jnp.sin(phase_screen[layer_index])
            lifted = jnp.stack([spread[0] * cosine_part - spread[1] * sine_part, spread[0] * sine_part + spread[1] * cosine_part])
            current = jnp.where(plane_index < slab_planes[slab_index], lifted, current)
    return current

def reference(incident, target, kernel, phase_screen, plane_shift, slab_planes):

    def loss_value(phases):
        difference = exit_field(phases, incident, kernel, plane_shift, slab_planes) - target
        return 0.5 * jnp.sum(difference * difference)
    return jax.grad(loss_value)(phase_screen)
```

```python
import functools
import math

import jax
import jax.numpy as jnp
from jax import lax
from jax.experimental import pallas as pl
from jax.experimental.pallas import tpu as pltpu
from jax.sharding import PartitionSpec as P

TILT_MAX = 8
REACH = 16
STEP = REACH + TILT_MAX
DEPTH = 3
MESH = pl.DeviceIdType.MESH
F32, BF16 = jnp.float32, jnp.bfloat16


def groups_of(count):
    out = [DEPTH] * (count // DEPTH)
    if count % DEPTH:
        out.append(count % DEPTH)
    return out


def split(value):
    high = value.astype(BF16)
    return high, (value - high.astype(F32)).astype(BF16)


def dot3(left, right):
    (lh, ll), (rh, rl) = left, right
    go = functools.partial(jnp.dot, preferred_element_type=F32)
    return go(lh, rh) + (go(lh, rl) + go(ll, rh))


def sin_cos(x):
    y = x * x
    sine, cosine = 0.0, 0.0
    for n in (13, 11, 9, 7, 5, 3, 1):
        sine = sine * y + (-1.0) ** (n // 2) / math.factorial(n)
    for n in (14, 12, 10, 8, 6, 4, 2, 0):
        cosine = cosine * y + (-1.0) ** (n // 2) / math.factorial(n)
    return sine * x, cosine


def body(cfg, taps, shifts, counts, incident, target, phases, out, *scratch):
    tiles, slabs, planes, rows, cols, live, fwd, bwd = cfg
    n_ex = len(fwd) + len(bwd)
    (row_m, col_m, ph, par, par_s, sines, cosines, saved, aim, mid, grads,
     own_sem, par_ssem, par_rsem, ph_ssem, ph_rsem, ex_ssem, ex_rsem, g_ssem, g_rsem,
     *fields) = scratch
    edge = ph.shape[2] - rows
    edge //= 2
    tile, slab = lax.axis_index("tile"), lax.axis_index("slab")
    worker = slab == 0
    has_low, has_high = tile > 0, tile < tiles - 1
    barrier = pltpu.get_barrier_semaphore()

    def greet(t, s):
        pl.semaphore_signal(barrier, inc=1, device_id={"tile": t, "slab": s}, device_id_type=MESH)

    @pl.when(worker)
    def _():
        for s in range(1, slabs):
            greet(tile, s)

        @pl.when(has_low)
        def _():
            for s in range(slabs):
                greet(tile - 1, s)

        @pl.when(has_high)
        def _():
            for s in range(slabs):
                greet(tile + 1, s)

    @pl.when(jnp.logical_not(worker))
    def _():
        greet(tile, 0)

    def remote(src, dst, ssem, rsem, t, s):
        return pltpu.make_async_remote_copy(
            src_ref=src, dst_ref=dst, send_sem=ssem, recv_sem=rsem,
            device_id={"tile": t, "slab": s}, device_id_type=MESH)

    def inc_up():
        h = fwd[0] * STEP
        return remote(incident.at[:, rows - h:, :], fields[0].at[:, 0:h, :],
                      ex_ssem.at[0], ex_rsem.at[0], tile + 1, 0)

    def inc_down():
        h = fwd[0] * STEP
        return remote(incident.at[:, 0:h, :], fields[0].at[:, h + rows:, :],
                      ex_ssem.at[1], ex_rsem.at[1], tile - 1, 0)

    def halo_up(e, h):
        return remote(fields[e].at[:, rows:rows + h, :], fields[e].at[:, 0:h, :],
                      ex_ssem.at[2 * e], ex_rsem.at[2 * e], tile + 1, 0)

    def halo_down(e, h):
        return remote(fields[e].at[:, h:2 * h, :], fields[e].at[:, h + rows:, :],
                      ex_ssem.at[2 * e + 1], ex_rsem.at[2 * e + 1], tile - 1, 0)

    def ph_mid(s):
        return remote(phases, ph.at[s, :, edge:edge + rows, :],
                      ph_ssem.at[0], ph_rsem.at[s, 0], tile, 0)

    def ph_up(s):
        return remote(phases.at[:, rows - edge:, :], ph.at[s, :, 0:edge, :],
                      ph_ssem.at[1], ph_rsem.at[s, 1], tile + 1, 0)

    def ph_down(s):
        return remote(phases.at[:, 0:edge, :], ph.at[s, :, edge + rows:, :],
                      ph_ssem.at[2], ph_rsem.at[s, 2], tile - 1, 0)

    def par_send(s):
        return remote(par.at[s], par.at[s], par_ssem, par_rsem.at[s], tile, 0)

    def grad_send(s):
        return remote(grads.at[s], out, g_ssem.at[s], g_rsem, tile, s)

    lane = lax.broadcasted_iota(jnp.int32, (8, cols), 1)
    own = jnp.where(lane == planes, counts[0], 0)
    for i in range(planes):
        own = jnp.where(lane == i, shifts[i], own)
    par[slab] = own

    h0 = fwd[0] * STEP
    local_inc = pltpu.make_async_copy(incident, fields[0].at[:, h0:h0 + rows, :], own_sem.at[0])
    local_ph = pltpu.make_async_copy(phases, ph.at[0, :, edge:edge + rows, :], own_sem.at[1])
    local_aim = pltpu.make_async_copy(target, aim, own_sem.at[2])
    local_par = pltpu.make_async_copy(par, par_s, own_sem.at[3])

    greeters = has_low.astype(jnp.int32) + has_high.astype(jnp.int32)
    pl.semaphore_wait(barrier, greeters + jnp.where(worker, slabs - 1, 1))

    @pl.when(worker & has_high)
    def _():
        inc_up().start()

    @pl.when(worker & has_low)
    def _():
        inc_down().start()

    @pl.when(jnp.logical_not(worker))
    def _():
        par_send(slab).start()
        ph_mid(slab).start()

    if edge:
        @pl.when(has_high)
        def _():
            ph_up(slab).start()

        @pl.when(has_low)
        def _():
            ph_down(slab).start()

    @pl.when(worker)
    def _():
        local_inc.start()
        local_ph.start()
        local_aim.start()

        def clear(has, low):
            @pl.when(jnp.logical_not(has))
            def _():
                for e, size in enumerate(fwd + bwd):
                    h = size * STEP
                    at = slice(0, h) if low else slice(h + rows, 2 * h + rows)
                    fields[e][:, at, :] = jnp.zeros((2, h, cols), F32)
                if edge:
                    at = slice(0, edge) if low else slice(edge + rows, 2 * edge + rows)
                    ph[:, :, at, :] = jnp.zeros((slabs, planes, edge, cols), F32)
        clear(has_low, True)
        clear(has_high, False)

        big, wide = row_m.shape[3:]

        def build(direction):
            sign = 1.0 if direction == 0 else -1.0
            at_row = lax.broadcasted_iota(jnp.int32, (8, wide), 1)
            at_col = lax.broadcasted_iota(jnp.int32, (8, cols), 1)
            band_r = [jnp.zeros((8, wide), F32)] * 2
            band_c = [jnp.zeros((8, cols), F32)] * 2
            for j in range(2 * REACH + 1):
                tap = j if direction == 0 else 2 * REACH - j
                off = REACH - j if direction == 0 else j - REACH
                off %= cols
                here, there = at_row == j, at_col == off
                for part in range(2):
                    gain = 1.0 if part == 0 else sign
                    band_r[part] = jnp.where(here, gain * taps[part, tap], band_r[part])
                    band_c[part] = jnp.where(there, gain * taps[part, j], band_c[part])
            for part in range(2):
                full = jnp.concatenate([band_r[part]] * (big // 8), axis=0)
                full = pltpu.roll(full, 0, 1, stride=1, stride_axis=0)
                row_m[direction, 0, part], row_m[direction, 1, part] = split(full)
            near = jnp.abs(lax.broadcasted_iota(jnp.int32, (cols, cols), 0)
                           - lax.broadcasted_iota(jnp.int32, (cols, cols), 1)) <= REACH
            real, imag = [
                jnp.where(near, pltpu.roll(jnp.concatenate([band_c[part]] * (cols // 8), axis=0),
                                           0, 1, stride=1, stride_axis=0), 0.0)
                for part in range(2)]
            block = jnp.concatenate([jnp.concatenate([real, imag], axis=1),
                                     jnp.concatenate([-imag, real], axis=1)], axis=0)
            col_m[direction, 0], col_m[direction, 1] = split(block)

        build(0)

        def spread(ref, start, count, direction):
            taken = count + 2 * REACH
            field = jnp.concatenate(
                [ref[0, pl.ds(start, taken), :], ref[1, pl.ds(start, taken), :]], axis=1)
            high, low = split(field)
            if taken < wide:
                rest = jnp.zeros((wide - taken, 2 * cols), BF16)
                high = jnp.concatenate([high, rest], axis=0)
                low = jnp.concatenate([low, rest], axis=0)
            matrix = [jnp.concatenate([row_m[direction, level, 0, 0:count, :],
                                       row_m[direction, level, 1, 0:count, :]], axis=0)
                      for level in range(2)]
            made = dot3(matrix, (high, low))
            top, low_half = made[:count], made[count:]
            field = jnp.concatenate([top[:, :cols] - low_half[:, cols:],
                                     top[:, cols:] + low_half[:, :cols]], axis=1)
            made = dot3(split(field), (col_m[direction, 0], col_m[direction, 1]))
            return made[:, :cols], made[:, cols:]

        def start_halos(e, h):
            @pl.when(has_high)
            def _():
                halo_up(e, h).start()

            @pl.when(has_low)
            def _():
                halo_down(e, h).start()

        def take_halos(e, h):
            @pl.when(has_low)
            def _():
                halo_up(e, h).wait_recv()

            @pl.when(has_high)
            def _():
                halo_down(e, h).wait_recv()

        for s in range(1, slabs):
            par_send(s).wait_recv()
        local_par.start()
        local_par.wait()
        key, before = [], 0
        for s in range(slabs):
            number = par_s[s, 0, planes]
            for i in range(planes):
                key.append(jnp.where(i < number, before + i, -1))
            before = before + number
        total = slabs * planes
        may_be = [[p for p in range(total)
                   if 0 <= p - k <= min(total - live, (p // planes) * (planes - 1))]
                  for k in range(live)]
        shift = []
        for k in range(live):
            value = 0
            for p in may_be[k]:
                value = jnp.where(key[p] == k, par_s[p // planes, 0, p % planes], value)
            shift.append(value)

        ext = rows + 2 * edge
        at = lax.broadcasted_iota(jnp.int32, (ext, cols), 0) + (tile * rows - edge)
        inside = (at >= 0) & (at < tiles * rows)
        arrived = [0]

        def ready(slab_needed):
            while arrived[0] <= slab_needed:
                s = arrived[0]
                if s == 0:
                    local_ph.wait()
                else:
                    ph_mid(s).wait_recv()
                if edge:
                    @pl.when(has_low)
                    def _():
                        ph_up(s).wait_recv()

                    @pl.when(has_high)
                    def _():
                        ph_down(s).wait_recv()
                arrived[0] += 1

        def trig(k):
            ready(may_be[k][-1] // planes)
            value = None
            for p in may_be[k]:
                one = ph[p // planes, p % planes]
                value = one if value is None else jnp.where(key[p] == k, one, value)
            sine, cosine = sin_cos(value)
            sines[k] = jnp.where(inside, sine, 0.0)
            cosines[k] = jnp.where(inside, cosine, 0.0)

        local_inc.wait()
        k = 0
        for e, size in enumerate(fwd):
            h = size * STEP
            if e:
                start_halos(e, h)
            if e == len(fwd) - 1:
                build(1)
            for j in range(size):
                if j == 0:
                    trig(k)
                    take_halos(e, h)
                more = STEP * (size - 1 - j)
                count = rows + 2 * more
                real, imag = spread(fields[e] if j == 0 else mid.at[k], 8 + shift[k], count, 0)
                if j:
                    trig(k)
                sine = sines[k, edge - more:edge - more + count, :]
                cosine = cosines[k, edge - more:edge - more + count, :]
                new_r, new_i = real * cosine - imag * sine, real * sine + imag * cosine
                if j < size - 1:
                    mid[k + 1, 0, 0:count, :] = new_r
                    mid[k + 1, 1, 0:count, :] = new_i
                own_r, own_i = new_r[more:more + rows], new_i[more:more + rows]
                saved[k, 0], saved[k, 1] = own_r, own_i
                if j == size - 1 and e + 1 < len(fwd):
                    g = fwd[e + 1] * STEP
                    fields[e + 1][0, g:g + rows, :] = own_r
                    fields[e + 1][1, g:g + rows, :] = own_i
                k += 1

        local_aim.wait()
        slopes = {}
        last = live - 1
        adj_r, adj_i = own_r - aim[0], own_i - aim[1]

        def slope(k, adj_r, adj_i):
            slopes[k] = saved[k, 0] * adj_i - saved[k, 1] * adj_r

        def weigh(k, adj_r, adj_i, more):
            span = slice(edge - more, edge + rows + more)
            sine, cosine = sines[k, span, :], cosines[k, span, :]
            return adj_r * cosine + adj_i * sine, adj_i * cosine - adj_r * sine

        sent = [slabs]

        def hand_out(k):
            while sent[0] > 0:
                s = sent[0] - 1
                if min(kk for kk in range(live) for p in may_be[kk] if p // planes == s) < k:
                    return
                for i in range(planes):
                    p = s * planes + i
                    value = jnp.zeros((rows, cols), F32)
                    for kk in range(live):
                        if p in may_be[kk]:
                            value = jnp.where(key[p] == kk, slopes[kk], value)
                    if s:
                        grads[s, i] = value
                    else:
                        out[i] = value
                if s:
                    grad_send(s).start()
                sent[0] = s

        k = last
        for b, size in enumerate(bwd):
            e = len(fwd) + b
            h = size * STEP
            real, imag = weigh(k, adj_r, adj_i, 0)
            fields[e][0, h:h + rows, :] = real
            fields[e][1, h:h + rows, :] = imag
            start_halos(e, h)
            slope(k, adj_r, adj_i)
            hand_out(k)
            take_halos(e, h)
            for j in range(size):
                more = STEP * (size - 1 - j)
                count = rows + 2 * more
                real, imag = spread(fields[e] if j == 0 else mid.at[live + k], 8 - shift[k], count, 1)
                k -= 1
                if j < size - 1:
                    new_r, new_i = weigh(k, real, imag, more)
                    mid[live + k, 0, 0:count, :] = new_r
                    mid[live + k, 1, 0:count, :] = new_i
                adj_r, adj_i = real[more:more + rows], imag[more:more + rows]
                if j < size - 1:
                    slope(k, adj_r, adj_i)
                    hand_out(k)
        slope(0, adj_r, adj_i)
        hand_out(0)

        for e, size in enumerate(fwd + bwd):
            @pl.when(has_high)
            def _():
                (inc_up() if e == 0 else halo_up(e, size * STEP)).wait_send()

            @pl.when(has_low)
            def _():
                (inc_down() if e == 0 else halo_down(e, size * STEP)).wait_send()
        for s in range(1, slabs):
            grad_send(s).wait_send()

    if edge:
        @pl.when(has_high)
        def _():
            ph_up(slab).wait_send()

        @pl.when(has_low)
        def _():
            ph_down(slab).wait_send()

    @pl.when(jnp.logical_not(worker))
    def _():
        par_send(slab).wait_send()
        ph_mid(slab).wait_send()
        grad_send(slab).wait_recv()


def solution(mesh):
    tiles, slabs = mesh.shape["tile"], mesh.shape["slab"]

    def local(incident, target, kernel, phase_screen, plane_shift, slab_planes):
        planes, rows, cols = phase_screen.shape
        live = slabs * planes * 3 // 4
        fwd, bwd = groups_of(live), groups_of(live - 1)
        edge = (max(fwd + bwd) - 1) * STEP
        big = rows + 2 * edge
        wide = -(-(big + 2 * REACH) // 128) * 128
        n_ex = len(fwd) + len(bwd)
        cfg = (tiles, slabs, planes, rows, cols, live, fwd, bwd)
        dma = pltpu.SemaphoreType.DMA
        vmem = pltpu.VMEM
        scratch = [
            vmem((2, 2, 2, big, wide), BF16),
            vmem((2, 2, 2 * cols, 2 * cols), BF16),
            vmem((slabs, planes, big, cols), F32),
            vmem((slabs, 8, cols), jnp.int32),
            pltpu.SMEM((slabs, 8, cols), jnp.int32),
            vmem((live, big, cols), F32),
            vmem((live, big, cols), F32),
            vmem((live, 2, rows, cols), F32),
            vmem((2, rows, cols), F32),
            vmem((2 * live, 2, big, cols), F32),
            vmem((slabs, planes, rows, cols), F32),
            dma((4,)), dma, dma((slabs,)), dma((3,)), dma((slabs, 3)),
            dma((2 * n_ex,)), dma((2 * n_ex,)), dma((slabs,)), dma,
        ] + [vmem((2, rows + 2 * size * STEP, cols), F32) for size in fwd + bwd]
        smem = pl.BlockSpec(memory_space=pltpu.SMEM)
        hbm = pl.BlockSpec(memory_space=pl.ANY)
        return pl.pallas_call(
            functools.partial(body, cfg),
            out_shape=jax.ShapeDtypeStruct((planes, rows, cols), F32),
            in_specs=[smem, smem, smem, hbm, hbm, hbm],
            out_specs=pl.BlockSpec(memory_space=pltpu.VMEM),
            scratch_shapes=scratch,
            compiler_params=pltpu.CompilerParams(
                collective_id=0, has_side_effects=True, vmem_limit_bytes=48 * 2**20),
            name="diffraction",
        )(kernel, plane_shift, slab_planes, incident, target, phase_screen)

    placed = (P(None, "tile", None), P(None, "tile", None), P(), P("slab", "tile", None),
              P("slab"), P("slab"))
    return jax.shard_map(local, mesh=mesh, in_specs=placed,
                         out_specs=P("slab", "tile", None), check_vma=False)
```

```python
import functools
import math

import jax
import jax.numpy as jnp
from jax import lax
from jax.experimental import pallas as pl
from jax.experimental.pallas import tpu as pltpu
from jax.sharding import PartitionSpec as P

TILT_MAX = 8
REACH = 16
STEP = REACH + TILT_MAX
AHEAD, BACK = 3, 3
MESH = pl.DeviceIdType.MESH
F32, BF16 = jnp.float32, jnp.bfloat16


def groups_of(count, depth):
    out = [depth] * (count // depth)
    if count % depth:
        out.append(count % depth)
    return out


def split(value):
    high = value.astype(BF16)
    return high, (value - high.astype(F32)).astype(BF16)


def dot3(left, right):
    (lh, ll), (rh, rl) = left, right
    go = functools.partial(jnp.dot, preferred_element_type=F32)
    return go(lh, rh) + (go(lh, rl) + go(ll, rh))


def sin_cos(x):
    y = x * x
    sine, cosine = 0.0, 0.0
    for n in (13, 11, 9, 7, 5, 3, 1):
        sine = sine * y + (-1.0) ** (n // 2) / math.factorial(n)
    for n in (14, 12, 10, 8, 6, 4, 2, 0):
        cosine = cosine * y + (-1.0) ** (n // 2) / math.factorial(n)
    return sine * x, cosine


def body(cfg, taps, shifts, counts, incident, target, phases, out, *scratch):
    tiles, slabs, planes, rows, cols, live, fwd, bwd, may_be, need, gated = cfg
    n_ex = len(fwd) + len(bwd)
    (row_m, col_m, ph, par, par_s, sines, cosines, saved, aim, mid, grads,
     own_sem, par_ssem, par_rsem, ph_ssem, ph_rsem, ex_ssem, ex_rsem, g_ssem, g_rsem, go_sem, ed_ssem, ed_rsem,
     *fields) = scratch
    edge = ph.shape[2] - rows
    edge //= 2
    tile, slab = lax.axis_index("tile"), lax.axis_index("slab")
    worker = slab == 0
    has_low, has_high = tile > 0, tile < tiles - 1
    barrier = pltpu.get_barrier_semaphore()

    def greet(t, s):
        pl.semaphore_signal(barrier, inc=1, device_id={"tile": t, "slab": s}, device_id_type=MESH)

    @pl.when(worker)
    def _():
        for s in range(1, slabs):
            greet(tile, s)

        @pl.when(has_low)
        def _():
            for s in range(slabs):
                greet(tile - 1, s)

        @pl.when(has_high)
        def _():
            for s in range(slabs):
                greet(tile + 1, s)

    @pl.when(jnp.logical_not(worker))
    def _():
        greet(tile, 0)

    def remote(src, dst, ssem, rsem, t, s):
        return pltpu.make_async_remote_copy(
            src_ref=src, dst_ref=dst, send_sem=ssem, recv_sem=rsem,
            device_id={"tile": t, "slab": s}, device_id_type=MESH)

    def inc_up():
        h = fwd[0] * STEP
        return remote(incident.at[:, rows - h:, :], fields[0].at[:, 0:h, :],
                      ex_ssem.at[0], ex_rsem.at[0], tile + 1, 0)

    def inc_down():
        h = fwd[0] * STEP
        return remote(incident.at[:, 0:h, :], fields[0].at[:, h + rows:, :],
                      ex_ssem.at[1], ex_rsem.at[1], tile - 1, 0)

    def halo_up(e, h):
        return remote(fields[e].at[:, rows:rows + h, :], fields[e].at[:, 0:h, :],
                      ex_ssem.at[2 * e], ex_rsem.at[2 * e], tile + 1, 0)

    def halo_down(e, h):
        return remote(fields[e].at[:, h:2 * h, :], fields[e].at[:, h + rows:, :],
                      ex_ssem.at[2 * e + 1], ex_rsem.at[2 * e + 1], tile - 1, 0)

    def ph_mid(s):
        return remote(phases, ph.at[s, :, edge:edge + rows, :],
                      ph_ssem, ph_rsem.at[s], tile, 0)

    def ph_up(p):
        s, i, w = p // planes, p % planes, need[p]
        return remote(phases.at[i, rows - w:, :], ph.at[s, i, edge - w:edge, :],
                      ed_ssem.at[i, 0], ed_rsem.at[p, 0], tile + 1, 0)

    def ph_down(p):
        s, i, w = p // planes, p % planes, need[p]
        return remote(phases.at[i, 0:w, :], ph.at[s, i, edge + rows:edge + rows + w, :],
                      ed_ssem.at[i, 1], ed_rsem.at[p, 1], tile - 1, 0)

    def par_send(s):
        return remote(par.at[s], par.at[s], par_ssem, par_rsem.at[s], tile, 0)

    def grad_send(s):
        return remote(grads.at[s], out, g_ssem.at[s], g_rsem, tile, s)

    lane = lax.broadcasted_iota(jnp.int32, (8, cols), 1)
    own = jnp.where(lane == planes, counts[0], 0)
    for i in range(planes):
        own = jnp.where(lane == i, shifts[i], own)
    par[slab] = own

    h0 = fwd[0] * STEP
    local_inc = pltpu.make_async_copy(incident, fields[0].at[:, h0:h0 + rows, :], own_sem.at[0])
    local_ph = pltpu.make_async_copy(phases, ph.at[0, :, edge:edge + rows, :], own_sem.at[1])
    local_aim = pltpu.make_async_copy(target, aim, own_sem.at[2])
    local_out = pltpu.make_async_copy(grads.at[0], out, own_sem.at[4])
    local_par = pltpu.make_async_copy(par, par_s, own_sem.at[3])

    greeters = has_low.astype(jnp.int32) + has_high.astype(jnp.int32)
    pl.semaphore_wait(barrier, greeters + jnp.where(worker, slabs - 1, 1))

    @pl.when(worker & has_high)
    def _():
        inc_up().start()

    @pl.when(worker & has_low)
    def _():
        inc_down().start()

    @pl.when(jnp.logical_not(worker))
    def _():
        par_send(slab).start()
        ph_mid(slab).start()

    def on_edges(list_of_planes, act):
        if list_of_planes:
            @pl.when(has_high)
            def _():
                for p in list_of_planes:
                    act(ph_up(p))

            @pl.when(has_low)
            def _():
                for p in list_of_planes:
                    act(ph_down(p))

    edged = [[p for p in range(s * planes, (s + 1) * planes) if need[p]] for s in range(slabs)]
    for s in range(slabs):
        @pl.when(slab == s)
        def _(s=s):
            on_edges([p for p in edged[s] if p not in gated], lambda copy: copy.start())
            later = [p for p in edged[s] if p in gated]
            if later:
                pl.semaphore_wait(go_sem, 1)
                on_edges(later, lambda copy: copy.start())

    @pl.when(worker)
    def _():
        local_inc.start()
        local_ph.start()
        local_aim.start()

        def clear(has, low):
            @pl.when(jnp.logical_not(has))
            def _():
                for e, size in enumerate(fwd + bwd):
                    h = size * STEP
                    at = slice(0, h) if low else slice(h + rows, 2 * h + rows)
                    fields[e][:, at, :] = jnp.zeros((2, h, cols), F32)
                if edge:
                    at = slice(0, edge) if low else slice(edge + rows, 2 * edge + rows)
                    ph[:, :, at, :] = jnp.zeros((slabs, planes, edge, cols), F32)
        clear(has_low, True)
        clear(has_high, False)

        big, wide = row_m.shape[3:]

        def build(direction):
            sign = 1.0 if direction == 0 else -1.0
            at_row = lax.broadcasted_iota(jnp.int32, (8, wide), 1)
            at_col = lax.broadcasted_iota(jnp.int32, (8, cols), 1)
            band_r = [jnp.zeros((8, wide), F32)] * 2
            band_c = [jnp.zeros((8, cols), F32)] * 2
            for j in range(2 * REACH + 1):
                tap = j if direction == 0 else 2 * REACH - j
                off = REACH - j if direction == 0 else j - REACH
                off %= cols
                here, there = at_row == j, at_col == off
                for part in range(2):
                    gain = 1.0 if part == 0 else sign
                    band_r[part] = jnp.where(here, gain * taps[part, tap], band_r[part])
                    band_c[part] = jnp.where(there, gain * taps[part, j], band_c[part])
            for part in range(2):
                full = jnp.concatenate([band_r[part]] * (big // 8), axis=0)
                full = pltpu.roll(full, 0, 1, stride=1, stride_axis=0)
                row_m[direction, 0, part], row_m[direction, 1, part] = split(full)
            near = jnp.abs(lax.broadcasted_iota(jnp.int32, (cols, cols), 0)
                           - lax.broadcasted_iota(jnp.int32, (cols, cols), 1)) <= REACH
            real, imag = [
                jnp.where(near, pltpu.roll(jnp.concatenate([band_c[part]] * (cols // 8), axis=0),
                                           0, 1, stride=1, stride_axis=0), 0.0)
                for part in range(2)]
            block = jnp.concatenate([jnp.concatenate([real, imag], axis=1),
                                     jnp.concatenate([-imag, real], axis=1)], axis=0)
            col_m[direction, 0], col_m[direction, 1] = split(block)

        build(0)

        def spread(ref, start, count, direction):
            taken = count + 2 * REACH
            field = jnp.concatenate(
                [ref[0, pl.ds(start, taken), :], ref[1, pl.ds(start, taken), :]], axis=1)
            high, low = split(field)
            if taken < wide:
                rest = jnp.zeros((wide - taken, 2 * cols), BF16)
                high = jnp.concatenate([high, rest], axis=0)
                low = jnp.concatenate([low, rest], axis=0)
            matrix = [jnp.concatenate([row_m[direction, level, 0, 0:count, :],
                                       row_m[direction, level, 1, 0:count, :]], axis=0)
                      for level in range(2)]
            made = dot3(matrix, (high, low))
            top, low_half = made[:count], made[count:]
            field = jnp.concatenate([top[:, :cols] - low_half[:, cols:],
                                     top[:, cols:] + low_half[:, :cols]], axis=1)
            made = dot3(split(field), (col_m[direction, 0], col_m[direction, 1]))
            return made[:, :cols], made[:, cols:]

        def start_halos(e, h):
            @pl.when(has_high)
            def _():
                halo_up(e, h).start()

            @pl.when(has_low)
            def _():
                halo_down(e, h).start()

        def take_halos(e, h):
            @pl.when(has_low)
            def _():
                halo_up(e, h).wait_recv()

            @pl.when(has_high)
            def _():
                halo_down(e, h).wait_recv()

        for s in range(1, slabs):
            par_send(s).wait_recv()
        local_par.start()
        local_par.wait()
        key, before = [], 0
        for s in range(slabs):
            number = par_s[s, 0, planes]
            for i in range(planes):
                key.append(jnp.where(i < number, before + i, -1))
            before = before + number
        shift = []
        for k in range(live):
            value = 0
            for p in may_be[k]:
                value = jnp.where(key[p] == k, par_s[p // planes, 0, p % planes], value)
            shift.append(value)

        ext = rows + 2 * edge
        at = lax.broadcasted_iota(jnp.int32, (ext, cols), 0) + (tile * rows - edge)
        inside = (at >= 0) & (at < tiles * rows)
        have_mid, have_edge = set(), set()

        def ready(some, mids, edges):
            for p in some:
                s = p // planes
                if mids and s not in have_mid:
                    have_mid.add(s)
                    if s == 0:
                        local_ph.wait()
                    else:
                        ph_mid(s).wait_recv()
                if edges and need[p] and p not in have_edge:
                    have_edge.add(p)

                    @pl.when(has_low)
                    def _():
                        ph_up(p).wait_recv()

                    @pl.when(has_high)
                    def _():
                        ph_down(p).wait_recv()

        def trig(k, low, high):
            ready(may_be[k], high > 0 and low < rows,
                  low < 0 or high > rows)
            span = slice(edge + low, edge + high)
            value = None
            for p in may_be[k]:
                one = ph[p // planes, p % planes, span, :]
                value = one if value is None else jnp.where(key[p] == k, one, value)
            sine, cosine = sin_cos(value)
            if low < 0 or high > rows:
                sine = jnp.where(inside[span], sine, 0.0)
                cosine = jnp.where(inside[span], cosine, 0.0)
            sines[k, span, :] = sine
            cosines[k, span, :] = cosine

        known = {}

        def widen(k, more):
            if k not in known:
                trig(k, -more, rows + more)
                known[k] = more
            elif known[k] < more:
                trig(k, -more, -known[k])
                trig(k, rows + known[k], rows + more)
                known[k] = more

        local_inc.wait()
        k = 0
        for e, size in enumerate(fwd):
            h = size * STEP
            if e:
                start_halos(e, h)
            if e == len(fwd) - 1:
                build(1)
            for j in range(size):
                more = STEP * (size - 1 - j)
                if j == 0:
                    if e:
                        widen(k, more)
                    take_halos(e, h)
                    if e == 0:
                        for s in sorted({p // planes for p in gated}):
                            pl.semaphore_signal(go_sem, inc=1, device_id={"tile": tile, "slab": s},
                                                device_id_type=MESH)
                count = rows + 2 * more
                real, imag = spread(fields[e] if j == 0 else mid.at[k], 8 + shift[k], count, 0)
                widen(k, more)
                sine = sines[k, edge - more:edge - more + count, :]
                cosine = cosines[k, edge - more:edge - more + count, :]
                new_r, new_i = real * cosine - imag * sine, real * sine + imag * cosine
                if j < size - 1:
                    mid[k + 1, 0, 0:count, :] = new_r
                    mid[k + 1, 1, 0:count, :] = new_i
                own_r, own_i = new_r[more:more + rows], new_i[more:more + rows]
                saved[k, 0], saved[k, 1] = own_r, own_i
                if j == size - 1 and e + 1 < len(fwd):
                    g = fwd[e + 1] * STEP
                    fields[e + 1][0, g:g + rows, :] = own_r
                    fields[e + 1][1, g:g + rows, :] = own_i
                k += 1

        local_aim.wait()
        slopes = {}
        last = live - 1
        adj_r, adj_i = own_r - aim[0], own_i - aim[1]

        def slope(k, adj_r, adj_i):
            slopes[k] = saved[k, 0] * adj_i - saved[k, 1] * adj_r

        def weigh(k, adj_r, adj_i, more):
            span = slice(edge - more, edge + rows + more)
            sine, cosine = sines[k, span, :], cosines[k, span, :]
            return adj_r * cosine + adj_i * sine, adj_i * cosine - adj_r * sine

        sent = [slabs]

        def hand_out(k):
            while sent[0] > 0:
                s = sent[0] - 1
                if min(kk for kk in range(live) for p in may_be[kk] if p // planes == s) < k:
                    return
                for i in range(planes):
                    p = s * planes + i
                    value = jnp.zeros((rows, cols), F32)
                    for kk in range(live):
                        if p in may_be[kk]:
                            value = jnp.where(key[p] == kk, slopes[kk], value)
                    grads[s, i] = value
                if s:
                    grad_send(s).start()
                else:
                    local_out.start()
                    local_out.wait()
                sent[0] = s

        k = last
        for b, size in enumerate(bwd):
            e = len(fwd) + b
            h = size * STEP
            real, imag = weigh(k, adj_r, adj_i, 0)
            fields[e][0, h:h + rows, :] = real
            fields[e][1, h:h + rows, :] = imag
            start_halos(e, h)
            slope(k, adj_r, adj_i)
            hand_out(k)
            for j in range(size - 1):
                widen(k - 1 - j, STEP * (size - 1 - j))
            take_halos(e, h)
            for j in range(size):
                more = STEP * (size - 1 - j)
                count = rows + 2 * more
                real, imag = spread(fields[e] if j == 0 else mid.at[live + k], 8 - shift[k], count, 1)
                k -= 1
                if j < size - 1:
                    new_r, new_i = weigh(k, real, imag, more)
                    mid[live + k, 0, 0:count, :] = new_r
                    mid[live + k, 1, 0:count, :] = new_i
                adj_r, adj_i = real[more:more + rows], imag[more:more + rows]
                if j < size - 1:
                    slope(k, adj_r, adj_i)
                    hand_out(k)
        slope(0, adj_r, adj_i)
        hand_out(0)

        ready(range(slabs * planes), True, True)
        for e, size in enumerate(fwd + bwd):
            @pl.when(has_high)
            def _():
                (inc_up() if e == 0 else halo_up(e, size * STEP)).wait_send()

            @pl.when(has_low)
            def _():
                (inc_down() if e == 0 else halo_down(e, size * STEP)).wait_send()
        for s in range(1, slabs):
            grad_send(s).wait_send()

    for s in range(slabs):
        @pl.when(slab == s)
        def _(s=s):
            on_edges(edged[s], lambda copy: copy.wait_send())

    @pl.when(jnp.logical_not(worker))
    def _():
        par_send(slab).wait_send()
        ph_mid(slab).wait_send()
        grad_send(slab).wait_recv()


def solution(mesh):
    tiles, slabs = mesh.shape["tile"], mesh.shape["slab"]

    def local(incident, target, kernel, phase_screen, plane_shift, slab_planes):
        planes, rows, cols = phase_screen.shape
        live = slabs * planes * 3 // 4
        fwd, bwd = groups_of(live, AHEAD), groups_of(live - 1, BACK)
        edge = (max(fwd + bwd) - 1) * STEP
        big = rows + 2 * edge
        wide = -(-(big + 2 * REACH) // 128) * 128
        n_ex = len(fwd) + len(bwd)
        total = slabs * planes
        may_be = [[p for p in range(total)
                   if 0 <= p - k <= min(total - live, (p // planes) * (planes - 1))]
                  for k in range(live)]
        used = [0] * live
        k = 0
        for size in fwd:
            for j in range(size):
                used[k] = STEP * (size - 1 - j)
                k += 1
        k = live - 1
        for size in bwd:
            for j in range(size):
                k -= 1
                if j < size - 1:
                    used[k] = max(used[k], STEP * (size - 1 - j))
        need = [max(used[k] for k in range(live) if p in may_be[k]) for p in range(total)]
        gated = [p for p in range(planes, total) if need[p] and
                 min(k for k in range(live) if p in may_be[k] and used[k]) >= fwd[0]]
        cfg = (tiles, slabs, planes, rows, cols, live, fwd, bwd, may_be, need, gated)
        dma = pltpu.SemaphoreType.DMA
        vmem = pltpu.VMEM
        scratch = [
            vmem((2, 2, 2, big, wide), BF16),
            vmem((2, 2, 2 * cols, 2 * cols), BF16),
            vmem((slabs, planes, big, cols), F32),
            vmem((slabs, 8, cols), jnp.int32),
            pltpu.SMEM((slabs, 8, cols), jnp.int32),
            vmem((live, big, cols), F32),
            vmem((live, big, cols), F32),
            vmem((live, 2, rows, cols), F32),
            vmem((2, rows, cols), F32),
            vmem((2 * live, 2, big, cols), F32),
            vmem((slabs, planes, rows, cols), F32),
            dma((5,)), dma, dma((slabs,)), dma, dma((slabs,)),
            dma((2 * n_ex,)), dma((2 * n_ex,)), dma((slabs,)), dma, pltpu.SemaphoreType.REGULAR,
            dma((planes, 2)), dma((slabs * planes, 2)),
        ] + [vmem((2, rows + 2 * size * STEP, cols), F32) for size in fwd + bwd]
        smem = pl.BlockSpec(memory_space=pltpu.SMEM)
        hbm = pl.BlockSpec(memory_space=pl.ANY)
        return pl.pallas_call(
            functools.partial(body, cfg),
            out_shape=jax.ShapeDtypeStruct((planes, rows, cols), F32),
            in_specs=[smem, smem, smem, hbm, hbm, hbm],
            out_specs=pl.BlockSpec(memory_space=pl.ANY),
            scratch_shapes=scratch,
            compiler_params=pltpu.CompilerParams(
                collective_id=0, has_side_effects=True, vmem_limit_bytes=55040 * 2**10),
            name="diffraction",
        )(kernel, plane_shift, slab_planes, incident, target, phase_screen)

    placed = (P(None, "tile", None), P(None, "tile", None), P(), P("slab", "tile", None),
              P("slab"), P("slab"))
    return jax.shard_map(local, mesh=mesh, in_specs=placed,
                         out_specs=P("slab", "tile", None), check_vma=False)
```
